32 devices in a mesh: frame: 4 (over z), panel: 8 (over y, x, core).
Axes of the slice: x: 2, y: 2, z: 4, core: 2. Of those that a mesh axis runs over, the one named last changes fastest.
Arguments:
- spline_index: int32 [4096, 2, 4, 256], P(('frame', 'panel')), may hold values from 0 to 124
- spline_frac: bfloat16 [4096, 2, 4, 256], P(('frame', 'panel')), may hold values from 0 to 1
- projection: bfloat16 [4096, 2, 4, 256], P(('frame', 'panel')), may hold values from -6 to 6
- forces: bfloat16 [4096, 256], P(('frame', 'panel')), may hold values from -6 to 6
- row_owner: int32 [4096, 1], P(('frame', 'panel')), may hold values from 0 to 31, as said below
- row_offset: int32 [4096], P(('frame', 'panel')), may hold values from 0 to 21
Outputs:
- normal_band: float32 [704, 2, 128, 128], P(('frame', 'panel'))
- normal_rhs: float32 [704, 128], P(('frame', 'panel'))
The draws below stay inside these ranges and needn't reach their ends.
Inputs may be any that keep to these rules, and one draw needn't show every extreme that they name: `row_owner`: among the row tiles of one device, no owner index is named by more than 8 tiles, and some owner index is named by exactly 8. Every owner index is named by some row tile.
All inputs are finite; a program needn't handle non-finite values.
Results may differ from the reference program's by a relative error of at most 0.0029.
Values may be sent and summed in bfloat16 or wider, within the bound.
A program may use at most 64 MiB of HBM per device.

```python
import jax
import jax.numpy as jnp
from jax import lax

CO = 128
BLK_DEV = 22
SLOTS = 2
NEI = 4
TR = 256
RT_DEV = 128
NBLK = 704
ROWTILES = 4096
CAP = 8
DEVICES = 32


def draw_row_owner(key, part):
    rows = jnp.arange(ROWTILES, dtype=jnp.int32)
    device_of = rows // RT_DEV
    within = rows % RT_DEV
    shuffled = jax.random.permutation(jax.random.fold_in(key, 11), DEVICES).astype(jnp.int32)
    owner = (shuffled[device_of] + within // CAP) % DEVICES
    return owner[:, None].astype(jnp.int32)


def draw_row_offset(key, part):
    rows = jnp.arange(ROWTILES, dtype=jnp.int32)
    within = rows % RT_DEV
    drawn = jax.random.randint(jax.random.fold_in(key, 23), (ROWTILES,), 0, BLK_DEV, dtype=jnp.int32)
    return jnp.where(within % CAP == 0, BLK_DEV - 1, drawn).astype(jnp.int32)


def plant(entries, stream_key, smallest, top_value):
    index_at = [jax.random.randint(jax.random.fold_in(stream_key, axis), (), 0, length) for axis, length in enumerate(entries.shape)]
    main_axis = entries.shape.index(max(entries.shape))
    next_to = index_at[:main_axis] + [(index_at[main_axis] + 1) % entries.shape[main_axis]] + index_at[main_axis + 1:]
    return entries.at[tuple(index_at)].set(smallest).at[tuple(next_to)].set(top_value)


def levels(key, extent, cuts, smallest, top_value):
    loudness, own = 1.0, jax.random.fold_in(key, 6)
    for dim, blocks in cuts:
        draws = jnp.exp(jax.random.uniform(jax.random.fold_in(own, dim), (blocks,), jnp.float32, smallest / len(cuts), top_value / len(cuts)))
        loudness = loudness * jnp.repeat(draws, extent[dim] // blocks).reshape([-1 if axis == dim else 1 for axis in range(len(extent))])
    return loudness


def centred(stream_key, dims, scale, bound, cuts=(), kind=jnp.bfloat16):
    factor_of = levels(stream_key, dims, cuts, -0.22, 0.18) if cuts else 1.0
    array = jax.random.normal(stream_key, dims, jnp.float32) * scale * factor_of
    return jnp.minimum(jnp.maximum(array, -bound), bound).astype(kind)


def setup_inputs(seed: int = 0) -> dict:
    seeds = jax.random.split(jax.random.key(seed), 7)
    return {
        "spline_index": plant(jax.random.randint(seeds[0], (ROWTILES, SLOTS, NEI, TR), 0, CO - 3), jax.random.fold_in(seeds[0], 1), 0, (CO - 3) - 1).astype(jnp.int32),
        "spline_frac": jnp.clip(1.0 * jax.random.uniform(seeds[1], (ROWTILES, SLOTS, NEI, TR), jnp.float32) ** levels(seeds[1], (ROWTILES, SLOTS, NEI, TR), ((0, 32),), -0.2, 0.2), 0.0, 1.0).astype(jnp.bfloat16),
        "projection": centred(seeds[2], (ROWTILES, SLOTS, NEI, TR), 1.0, 6.0, ((0, 32),)),
        "forces": centred(seeds[3], (ROWTILES, TR), 1.0, 6.0, ((0, 32),)),
        "row_owner": draw_row_owner(jax.random.fold_in(seeds[6], 71), 0),
        "row_offset": draw_row_offset(jax.random.fold_in(seeds[6], 71), 0),
    }


def basis_tiles(spline_index, spline_frac, projection, column_count):
    columns = lax.broadcasted_iota(jnp.int32, (1, 1, 1, column_count), 3)
    summed = jnp.zeros(spline_index.shape[:2] + (spline_index.shape[3], column_count), jnp.float32)
    for neighbor in range(spline_index.shape[2]):
        offset = columns - spline_index[:, :, neighbor, :, None]
        position = spline_frac[:, :, neighbor, :, None].astype(jnp.float32)
        weight = projection[:, :, neighbor, :, None].astype(jnp.float32)
        one_minus = 1.0 - position
        pos_square = position * position
        pos_cube = pos_square * position
        basis_zero = one_minus * one_minus * one_minus / 6.0
        basis_one = (3.0 * pos_cube - 6.0 * pos_square + 4.0) / 6.0
        basis_two = (-3.0 * pos_cube + 3.0 * pos_square + 3.0 * position + 1.0) / 6.0
        basis_three = pos_cube / 6.0
        basis_value = jnp.where(offset == 0, basis_zero,
                      jnp.where(offset == 1, basis_one,
                      jnp.where(offset == 2, basis_two,
                      jnp.where(offset == 3, basis_three, 0.0))))
        summed = summed + weight * basis_value
    return summed.astype(jnp.bfloat16)


def reference(spline_index, spline_frac, projection, forces, row_owner, row_offset):
    total_rows = spline_index.shape[0]
    slot_width = spline_index.shape[1]
    start = (row_owner[:, 0] * BLK_DEV + row_offset).astype(jnp.int32)
    batch_size = 256 if total_rows % 256 == 0 else total_rows
    turns = total_rows // batch_size

    def split(member):
        return member.reshape((turns, batch_size) + member.shape[1:])

    def accumulate(totals, pieces):
        band_acc, rhs_acc = totals
        index_part, frac_part, proj_part, force_part, start_part = pieces
        design = basis_tiles(index_part, frac_part, proj_part, CO).astype(jnp.float32)
        for band_lag in range(slot_width):
            left_tiles = design[:, :slot_width - band_lag]
            right_tiles = design[:, band_lag:]
            products = jnp.einsum("bsxi,bsxj->bsij", left_tiles, right_tiles,
                                  precision=lax.Precision.HIGHEST)
            rows_at = (start_part[:, None] + jnp.arange(slot_width - band_lag, dtype=jnp.int32)[None, :]) % NBLK
            band_acc = band_acc.at[rows_at, band_lag].add(products)
        moments = jnp.einsum("bsxi,bx->bsi", design, force_part.astype(jnp.float32),
                             precision=lax.Precision.HIGHEST)
        rows_all = (start_part[:, None] + jnp.arange(slot_width, dtype=jnp.int32)[None, :]) % NBLK
        rhs_acc = rhs_acc.at[rows_all].add(moments)
        return (band_acc, rhs_acc), None

    band_init = jnp.zeros((NBLK, slot_width, CO, CO), jnp.float32)
    rhs_init = jnp.zeros((NBLK, CO), jnp.float32)
    (normal_band, normal_rhs), unused = lax.scan(
        accumulate, (band_init, rhs_init),
        (split(spline_index), split(spline_frac), split(projection), split(forces), split(start)))
    return normal_band, normal_rhs
```

```python
import functools

import jax
import jax.numpy as jnp
from jax import lax
from jax.experimental import pallas as pl
from jax.experimental.pallas import tpu as pltpu
from jax.sharding import PartitionSpec as P

CO = 128
BLK_DEV = 22
PARTS = 1
GROUP = 16
ACC_ROWS = BLK_DEV + 3
TRASH = BLK_DEV + 1
HEAD = 16
AXES = ("frame", "panel")


def normal_kernel(terms, width, where_ref, rows_ref, *refs):
    if len(refs) == 12:
        band_in, rhs_in = refs[:2]
        refs = refs[2:]
    else:
        band_in = rhs_in = None
    band_ref, rhs_ref, index_ref, weight_ref, force_ref, even_ref, odd_ref, list_ref, block_ref = refs[:9]
    slots = rows_ref.shape[0]
    span = terms * width
    lanes = width // 128
    neighbors = terms // 2

    if band_in is None:
        band_ref[...] = jnp.zeros_like(band_ref)
        rhs_ref[...] = jnp.zeros_like(rhs_ref)
    else:
        band_ref[...] = band_in[...]
        rhs_ref[...] = rhs_in[...]

    def gather_list(slot, count):
        filled = where_ref[slot]
        list_ref[count] = slot
        block_ref[count] = filled - 1
        return count + (filled > 0).astype(jnp.int32)

    count = lax.fori_loop(0, slots, gather_list, jnp.int32(0))
    list_ref[count] = 0
    block_ref[count] = TRASH

    @pl.loop(0, slots // GROUP)
    def dense(group):
        at = pl.ds(pl.multiple_of(group * GROUP, GROUP), GROUP)
        for col in range(span // 128):
            index_ref[col, at, :] = rows_ref[at, pl.ds(col * 128, 128)].astype(jnp.float32).astype(jnp.int32)
            t = rows_ref[at, pl.ds(span + col * 128, 128)].astype(jnp.float32)
            p = rows_ref[at, pl.ds(2 * span + col * 128, 128)].astype(jnp.float32) * (1.0 / 6.0)
            one = 1.0 - t
            square = t * t
            cube = square * t
            weight_ref[0, col, at, :] = p * (one * one * one)
            weight_ref[1, col, at, :] = p * (3.0 * cube - 6.0 * square + 4.0)
            weight_ref[2, col, at, :] = p * (3.0 * (square - cube + t) + 1.0)
            weight_ref[3, col, at, :] = p * cube
        for lane in range(lanes):
            force_ref[lane, at, :] = rows_ref[at, pl.ds(3 * span + lane * 128, 128)].astype(jnp.float32)

    sub = lax.broadcasted_iota(jnp.int32, (8, 128), 0)

    def build(slot, design_ref):
        at = pl.ds(slot, 1)
        for lane in range(lanes):
            force = jnp.broadcast_to(force_ref[lane, at, :], (HEAD, 128)).astype(jnp.bfloat16)
            design_ref[0:HEAD, lane * 128 : lane * 128 + 128] = force
        for s in range(2):
            for lane in range(lanes):
                tiles = [None] * (CO // 8)
                for n in range(neighbors):
                    col = (s * neighbors + n) * lanes + lane
                    index = jnp.broadcast_to(index_ref[col, at, :], (8, 128))
                    m = (sub - index) & 7
                    value = jnp.where(m == 3, jnp.broadcast_to(weight_ref[3, col, at, :], (8, 128)), 0.0)
                    for k in (2, 1, 0):
                        value = jnp.where(m == k, jnp.broadcast_to(weight_ref[k, col, at, :], (8, 128)), value)
                    target = (index + m) >> 3
                    for a in range(CO // 8):
                        part = jnp.where(target == a, value, 0.0)
                        tiles[a] = part if tiles[a] is None else tiles[a] + part
                for a in range(0, CO // 8, 2):
                    pair = jnp.concatenate([tiles[a], tiles[a + 1]], axis=0).astype(jnp.bfloat16)
                    design_ref[HEAD + s * CO + a * 8 : HEAD + s * CO + a * 8 + 16, lane * 128 : lane * 128 + 128] = pair

    contract = (((1,), (1,)), ((), ()))

    def add(block, design_ref):
        top = lax.dot_general(
            design_ref[0 : HEAD + CO, :], design_ref[HEAD:, :], contract, preferred_element_type=jnp.float32
        )
        low = lax.dot_general(
            design_ref[HEAD + CO :, :], design_ref[HEAD + CO :, :], contract, preferred_element_type=jnp.float32
        )
        band_ref[block, 0] += top[HEAD:, :CO]
        band_ref[block, 1] += top[HEAD:, CO:]
        band_ref[block + 1, 0] += low
        rhs_ref[block] += top[0:8, :CO]
        rhs_ref[block + 1] += top[0:8, CO:]

    odd_ref[...] = jnp.zeros_like(odd_ref)

    def pair(step, before):
        first = 2 * step
        build(list_ref[first], even_ref)
        add(before, odd_ref)
        build(list_ref[first + 1], odd_ref)
        add(block_ref[first], even_ref)
        return block_ref[first + 1]

    last = lax.fori_loop(0, (count + 1) // 2, pair, jnp.int32(TRASH))
    add(last, odd_ref)


def normal_sums(where, rows, terms, width, totals):
    slots = rows.shape[0]
    span = terms * width
    vmem = pl.BlockSpec(memory_space=pltpu.VMEM)
    smem = pl.BlockSpec(memory_space=pltpu.SMEM)
    carried = () if totals is None else totals
    return pl.pallas_call(
        functools.partial(normal_kernel, terms, width),
        out_shape=(
            jax.ShapeDtypeStruct((ACC_ROWS, 2, CO, CO), jnp.float32),
            jax.ShapeDtypeStruct((ACC_ROWS, 8, CO), jnp.float32),
        ),
        in_specs=[smem, vmem] + [vmem] * len(carried),
        out_specs=(vmem, vmem),
        scratch_shapes=[
            pltpu.VMEM((span // 128, slots, 128), jnp.int32),
            pltpu.VMEM((4, span // 128, slots, 128), jnp.float32),
            pltpu.VMEM((width // 128, slots, 128), jnp.float32),
            pltpu.VMEM((HEAD + 2 * CO, width), jnp.bfloat16),
            pltpu.VMEM((HEAD + 2 * CO, width), jnp.bfloat16),
            pltpu.SMEM((slots + 8,), jnp.int32),
            pltpu.SMEM((slots + 8,), jnp.int32),
        ],
        compiler_params=pltpu.CompilerParams(vmem_limit_bytes=40 * 1024 * 1024),
        cost_estimate=pl.CostEstimate(
            flops=slots * 20 * 1000 * 1000 * width // 256, bytes_accessed=10 * 1000 * 1000, transcendentals=0
        ),
    )(where, rows, *carried)


def on_device(spline_index, spline_frac, projection, forces, row_owner, row_offset):
    row_count, slot_width, neighbors, design_rows = spline_index.shape
    terms = slot_width * neighbors
    device_count = lax.axis_size(AXES)
    capacity = max(2, 2 * row_count // device_count)
    slot_count = device_count * capacity
    width = design_rows // PARTS

    owners = row_owner[:, 0]
    same_owner = owners[:, None] == owners[None, :]
    row_at = lax.broadcasted_iota(jnp.int32, (row_count, row_count), 0)
    other_at = lax.broadcasted_iota(jnp.int32, (row_count, row_count), 1)
    position = jnp.sum((same_owner & (other_at < row_at)).astype(jnp.int32), axis=1)
    target = owners * capacity + position
    chosen = (lax.broadcasted_iota(jnp.int32, (slot_count, row_count), 0) == target[None, :]).astype(jnp.bfloat16)
    tag = jnp.broadcast_to((row_offset + 1).astype(jnp.bfloat16)[:, None], (row_count, 128))

    received = []
    for part in range(PARTS):
        cut = slice(part * width, (part + 1) * width)
        payload = jnp.concatenate(
            [
                spline_index[..., cut].astype(jnp.bfloat16).reshape(row_count, terms * width),
                spline_frac[..., cut].reshape(row_count, terms * width),
                projection[..., cut].reshape(row_count, terms * width),
                forces[:, cut],
                tag,
            ],
            axis=1,
        )
        outgoing = jnp.dot(chosen, payload, preferred_element_type=jnp.bfloat16)
        received.append(lax.all_to_all(outgoing, AXES, split_axis=0, concat_axis=0, tiled=True))

    totals = None
    for rows in received:
        where = rows[:, 3 * terms * width + width].astype(jnp.int32)
        totals = normal_sums(where, rows, terms, width, totals)
    band, rhs = totals
    rhs = rhs[:, 0]
    spill = jnp.concatenate([band[BLK_DEV, 0], rhs[BLK_DEV : BLK_DEV + 1]], axis=0)
    route = [(i, (i + 1) % device_count) for i in range(device_count)]
    spill = lax.ppermute(spill, AXES, route)
    normal_band = band[:BLK_DEV].at[0, 0].add(spill[:CO])
    normal_rhs = rhs[:BLK_DEV].at[0].add(spill[CO])
    return (normal_band, normal_rhs)


def solution(mesh):
    split = P(AXES)
    return jax.shard_map(
        on_device, mesh=mesh, in_specs=(split,) * 6, out_specs=(split, split), check_vma=False
    )
```

```python
import functools

import jax
import jax.numpy as jnp
from jax import lax
from jax.experimental import pallas as pl
from jax.experimental.pallas import tpu as pltpu
from jax.sharding import PartitionSpec as P

CO = 128
BLK_DEV = 22
GROUP = 16
ACC_ROWS = BLK_DEV + 3
TRASH = BLK_DEV + 1
HEAD = 16
AXES = ("frame", "panel")


def normal_kernel(terms, width, where_ref, rows_ref, *refs):
    if len(refs) == 11:
        band_in, rhs_in = refs[:2]
        refs = refs[2:]
    else:
        band_in = rhs_in = None
    band_ref, rhs_ref, index_ref, weight_ref, force_ref, even_ref, odd_ref, list_ref, block_ref = refs
    slots = rows_ref.shape[0]
    span = terms * width
    lanes = width // 128
    neighbors = terms // 2

    if band_in is None:
        band_ref[...] = jnp.zeros_like(band_ref)
        rhs_ref[...] = jnp.zeros_like(rhs_ref)
    else:
        band_ref[...] = band_in[...]
        rhs_ref[...] = rhs_in[...]

    def gather_list(slot, count):
        filled = where_ref[slot]
        list_ref[count] = slot
        block_ref[count] = filled - 1
        return count + (filled > 0).astype(jnp.int32)

    count = lax.fori_loop(0, slots, gather_list, jnp.int32(0))
    list_ref[count] = 0
    block_ref[count] = TRASH

    @pl.loop(0, slots // GROUP)
    def dense(group):
        at = pl.ds(pl.multiple_of(group * GROUP, GROUP), GROUP)
        for col in range(span // 128):
            index_ref[col, at, :] = rows_ref[at, pl.ds(col * 128, 128)].astype(jnp.float32).astype(jnp.int32)
            t = rows_ref[at, pl.ds(span + col * 128, 128)].astype(jnp.float32)
            p = rows_ref[at, pl.ds(2 * span + col * 128, 128)].astype(jnp.float32) * (1.0 / 6.0)
            one = 1.0 - t
            square = t * t
            cube = square * t
            weight_ref[0, col, at, :] = p * (one * one * one)
            weight_ref[1, col, at, :] = p * (3.0 * cube - 6.0 * square + 4.0)
            weight_ref[2, col, at, :] = p * (3.0 * (square - cube + t) + 1.0)
            weight_ref[3, col, at, :] = p * cube
        for lane in range(lanes):
            force_ref[lane, at, :] = rows_ref[at, pl.ds(3 * span + lane * 128, 128)].astype(jnp.float32)

    sub = lax.broadcasted_iota(jnp.int32, (8, 128), 0)

    def build(slot, design_ref):
        at = pl.ds(slot, 1)
        for lane in range(lanes):
            force = jnp.broadcast_to(force_ref[lane, at, :], (HEAD, 128)).astype(jnp.bfloat16)
            design_ref[0:HEAD, lane * 128 : lane * 128 + 128] = force
        for s in range(2):
            for lane in range(lanes):
                tiles = [None] * (CO // 8)
                for n in range(neighbors):
                    col = (s * neighbors + n) * lanes + lane
                    index = jnp.broadcast_to(index_ref[col, at, :], (8, 128))
                    m = (sub - index) & 7
                    value = jnp.where(m == 3, jnp.broadcast_to(weight_ref[3, col, at, :], (8, 128)), 0.0)
                    for k in (2, 1, 0):
                        value = jnp.where(m == k, jnp.broadcast_to(weight_ref[k, col, at, :], (8, 128)), value)
                    target = (index + m) >> 3
                    for a in range(CO // 8):
                        part = jnp.where(target == a, value, 0.0)
                        tiles[a] = part if tiles[a] is None else tiles[a] + part
                for a in range(0, CO // 8, 2):
                    pair = jnp.concatenate([tiles[a], tiles[a + 1]], axis=0).astype(jnp.bfloat16)
                    design_ref[HEAD + s * CO + a * 8 : HEAD + s * CO + a * 8 + 16, lane * 128 : lane * 128 + 128] = pair

    contract = (((1,), (1,)), ((), ()))

    def add(block, design_ref):
        top = lax.dot_general(
            design_ref[0 : HEAD + CO, :], design_ref[HEAD:, :], contract, preferred_element_type=jnp.float32
        )
        low = lax.dot_general(
            design_ref[HEAD + CO :, :], design_ref[HEAD + CO :, :], contract, preferred_element_type=jnp.float32
        )
        band_ref[block, 0] += top[HEAD:, :CO]
        band_ref[block, 1] += top[HEAD:, CO:]
        band_ref[block + 1, 0] += low
        rhs_ref[block] += top[0:8, :CO]
        rhs_ref[block + 1] += top[0:8, CO:]

    odd_ref[...] = jnp.zeros_like(odd_ref)

    def pair(step, before):
        first = 2 * step
        build(list_ref[first], even_ref)
        add(before, odd_ref)
        build(list_ref[first + 1], odd_ref)
        add(block_ref[first], even_ref)
        return block_ref[first + 1]

    last = lax.fori_loop(0, (count + 1) // 2, pair, jnp.int32(TRASH))
    add(last, odd_ref)


def normal_sums(where, rows, terms, width, totals):
    slots = rows.shape[0]
    span = terms * width
    vmem = pl.BlockSpec(memory_space=pltpu.VMEM)
    smem = pl.BlockSpec(memory_space=pltpu.SMEM)
    carried = () if totals is None else totals
    return pl.pallas_call(
        functools.partial(normal_kernel, terms, width),
        out_shape=(
            jax.ShapeDtypeStruct((ACC_ROWS, 2, CO, CO), jnp.float32),
            jax.ShapeDtypeStruct((ACC_ROWS, 8, CO), jnp.float32),
        ),
        in_specs=[smem, vmem] + [vmem] * len(carried),
        out_specs=(vmem, vmem),
        scratch_shapes=[
            pltpu.VMEM((span // 128, slots, 128), jnp.int32),
            pltpu.VMEM((4, span // 128, slots, 128), jnp.float32),
            pltpu.VMEM((width // 128, slots, 128), jnp.float32),
            pltpu.VMEM((HEAD + 2 * CO, width), jnp.bfloat16),
            pltpu.VMEM((HEAD + 2 * CO, width), jnp.bfloat16),
            pltpu.SMEM((slots + 8,), jnp.int32),
            pltpu.SMEM((slots + 8,), jnp.int32),
        ],
        compiler_params=pltpu.CompilerParams(vmem_limit_bytes=40 * 1024 * 1024),
        cost_estimate=pl.CostEstimate(
            flops=slots * 20 * 1000 * 1000 * width // 256, bytes_accessed=10 * 1000 * 1000, transcendentals=0
        ),
    )(where, rows, *carried)


def on_device(spline_index, spline_frac, projection, forces, row_owner, row_offset):
    row_count, slot_width, neighbors, design_rows = spline_index.shape
    terms = slot_width * neighbors
    device_count = lax.axis_size(AXES)
    capacity = max(2, 2 * row_count // device_count)
    width = design_rows
    waves = [size for size in (capacity // 2, capacity // 4, capacity - capacity // 2 - capacity // 4) if size]

    owners = row_owner[:, 0]
    same_owner = owners[:, None] == owners[None, :]
    row_at = lax.broadcasted_iota(jnp.int32, (row_count, row_count), 0)
    other_at = lax.broadcasted_iota(jnp.int32, (row_count, row_count), 1)
    position = jnp.sum((same_owner & (other_at < row_at)).astype(jnp.int32), axis=1)
    tag = jnp.broadcast_to((row_offset + 1).astype(jnp.bfloat16)[:, None], (row_count, 128))
    payload = jnp.concatenate(
        [
            spline_index.astype(jnp.bfloat16).reshape(row_count, terms * width),
            spline_frac.reshape(row_count, terms * width),
            projection.reshape(row_count, terms * width),
            forces,
            tag,
        ],
        axis=1,
    )

    received = []
    first = 0
    for size in waves:
        slot_at = lax.broadcasted_iota(jnp.int32, (device_count * size, row_count), 0)
        chosen = (slot_at // size == owners[None, :]) & (slot_at % size + first == position[None, :])
        outgoing = jnp.dot(chosen.astype(jnp.bfloat16), payload, preferred_element_type=jnp.bfloat16)
        received.append(lax.all_to_all(outgoing, AXES, split_axis=0, concat_axis=0, tiled=True))
        first += size

    totals = None
    for rows in received:
        where = rows[:, 3 * terms * width + width].astype(jnp.int32)
        totals = normal_sums(where, rows, terms, width, totals)
    band, rhs = totals
    rhs = rhs[:, 0]
    spill = jnp.concatenate([band[BLK_DEV, 0], rhs[BLK_DEV : BLK_DEV + 1]], axis=0)
    route = [(i, (i + 1) % device_count) for i in range(device_count)]
    spill = lax.ppermute(spill, AXES, route)
    normal_band = band[:BLK_DEV].at[0, 0].add(spill[:CO])
    normal_rhs = rhs[:BLK_DEV].at[0].add(spill[CO])
    return (normal_band, normal_rhs)


def solution(mesh):
    split = P(AXES)
    return jax.shard_map(
        on_device, mesh=mesh, in_specs=(split,) * 6, out_specs=(split, split), check_vma=False
    )
```

```python
import functools

import jax
import jax.numpy as jnp
from jax import lax
from jax.experimental import pallas as pl
from jax.experimental.pallas import tpu as pltpu
from jax.sharding import PartitionSpec as P

CO = 128
BLK_DEV = 22
GROUP = 16
ACC_ROWS = BLK_DEV + 3
TRASH = BLK_DEV + 1
HEAD = 16
AXES = ("frame", "panel")


def normal_kernel(terms, width, pick, where_ref, rows_ref, *refs):
    if len(refs) == 11:
        band_in, rhs_in = refs[:2]
        refs = refs[2:]
    else:
        band_in = rhs_in = None
    band_ref, rhs_ref, index_ref, weight_ref, force_ref, even_ref, odd_ref, list_ref, block_ref = refs
    slots = rows_ref.shape[0]
    span = terms * width
    lanes = width // 128
    neighbors = terms // 2

    if band_in is None:
        band_ref[...] = jnp.zeros_like(band_ref)
        rhs_ref[...] = jnp.zeros_like(rhs_ref)
    else:
        band_ref[...] = band_in[...]
        rhs_ref[...] = rhs_in[...]

    def gather_list(slot, count):
        filled = where_ref[slot]
        list_ref[count] = slot
        block_ref[count] = filled - 1
        wanted = filled > 0
        if pick == "last":
            wanted = filled == BLK_DEV
        elif pick == "others":
            wanted = wanted & (filled != BLK_DEV)
        return count + wanted.astype(jnp.int32)

    count = lax.fori_loop(0, slots, gather_list, jnp.int32(0))
    list_ref[count] = 0
    block_ref[count] = TRASH

    @pl.loop(0, jnp.where(count > 0, slots // GROUP, 0))
    def dense(group):
        at = pl.ds(pl.multiple_of(group * GROUP, GROUP), GROUP)
        for col in range(span // 128):
            index_ref[col, at, :] = rows_ref[at, pl.ds(col * 128, 128)].astype(jnp.float32).astype(jnp.int32)
            t = rows_ref[at, pl.ds(span + col * 128, 128)].astype(jnp.float32)
            p = rows_ref[at, pl.ds(2 * span + col * 128, 128)].astype(jnp.float32) * (1.0 / 6.0)
            one = 1.0 - t
            square = t * t
            cube = square * t
            weight_ref[0, col, at, :] = p * (one * one * one)
            weight_ref[1, col, at, :] = p * (3.0 * cube - 6.0 * square + 4.0)
            weight_ref[2, col, at, :] = p * (3.0 * (square - cube + t) + 1.0)
            weight_ref[3, col, at, :] = p * cube
        for lane in range(lanes):
            force_ref[lane, at, :] = rows_ref[at, pl.ds(3 * span + lane * 128, 128)].astype(jnp.float32)

    sub = lax.broadcasted_iota(jnp.int32, (8, 128), 0)

    def build(slot, design_ref):
        at = pl.ds(slot, 1)
        for lane in range(lanes):
            force = jnp.broadcast_to(force_ref[lane, at, :], (HEAD, 128)).astype(jnp.bfloat16)
            design_ref[0:HEAD, lane * 128 : lane * 128 + 128] = force
        for s in range(2):
            for lane in range(lanes):
                tiles = [None] * (CO // 8)
                for n in range(neighbors):
                    col = (s * neighbors + n) * lanes + lane
                    index = jnp.broadcast_to(index_ref[col, at, :], (8, 128))
                    m = (sub - index) & 7
                    value = jnp.where(m == 3, jnp.broadcast_to(weight_ref[3, col, at, :], (8, 128)), 0.0)
                    for k in (2, 1, 0):
                        value = jnp.where(m == k, jnp.broadcast_to(weight_ref[k, col, at, :], (8, 128)), value)
                    target = (index + m) >> 3
                    for a in range(CO // 8):
                        part = jnp.where(target == a, value, 0.0)
                        tiles[a] = part if tiles[a] is None else tiles[a] + part
                for a in range(0, CO // 8, 2):
                    pair = jnp.concatenate([tiles[a], tiles[a + 1]], axis=0).astype(jnp.bfloat16)
                    design_ref[HEAD + s * CO + a * 8 : HEAD + s * CO + a * 8 + 16, lane * 128 : lane * 128 + 128] = pair

    contract = (((1,), (1,)), ((), ()))

    def add(block, design_ref):
        top = lax.dot_general(
            design_ref[0 : HEAD + CO, :], design_ref[HEAD:, :], contract, preferred_element_type=jnp.float32
        )
        low = lax.dot_general(
            design_ref[HEAD + CO :, :], design_ref[HEAD + CO :, :], contract, preferred_element_type=jnp.float32
        )
        band_ref[block, 0] += top[HEAD:, :CO]
        band_ref[block, 1] += top[HEAD:, CO:]
        band_ref[block + 1, 0] += low
        rhs_ref[block] += top[0:8, :CO]
        rhs_ref[block + 1] += top[0:8, CO:]

    odd_ref[...] = jnp.zeros_like(odd_ref)

    def pair(step, before):
        first = 2 * step
        build(list_ref[first], even_ref)
        add(before, odd_ref)
        build(list_ref[first + 1], odd_ref)
        add(block_ref[first], even_ref)
        return block_ref[first + 1]

    last = lax.fori_loop(0, (count + 1) // 2, pair, jnp.int32(TRASH))
    add(last, odd_ref)


def normal_sums(where, rows, terms, width, totals, pick):
    slots = rows.shape[0]
    span = terms * width
    vmem = pl.BlockSpec(memory_space=pltpu.VMEM)
    smem = pl.BlockSpec(memory_space=pltpu.SMEM)
    carried = () if totals is None else totals
    return pl.pallas_call(
        functools.partial(normal_kernel, terms, width, pick),
        out_shape=(
            jax.ShapeDtypeStruct((ACC_ROWS, 2, CO, CO), jnp.float32),
            jax.ShapeDtypeStruct((ACC_ROWS, 8, CO), jnp.float32),
        ),
        in_specs=[smem, vmem] + [vmem] * len(carried),
        out_specs=(vmem, vmem),
        scratch_shapes=[
            pltpu.VMEM((span // 128, slots, 128), jnp.int32),
            pltpu.VMEM((4, span // 128, slots, 128), jnp.float32),
            pltpu.VMEM((width // 128, slots, 128), jnp.float32),
            pltpu.VMEM((HEAD + 2 * CO, width), jnp.bfloat16),
            pltpu.VMEM((HEAD + 2 * CO, width), jnp.bfloat16),
            pltpu.SMEM((slots + 8,), jnp.int32),
            pltpu.SMEM((slots + 8,), jnp.int32),
        ],
        compiler_params=pltpu.CompilerParams(vmem_limit_bytes=40 * 1024 * 1024),
        cost_estimate=pl.CostEstimate(
            flops=slots * 20 * 1000 * 1000 * width // 256, bytes_accessed=10 * 1000 * 1000, transcendentals=0
        ),
    )(where, rows, *carried)


def on_device(spline_index, spline_frac, projection, forces, row_owner, row_offset):
    row_count, slot_width, neighbors, design_rows = spline_index.shape
    terms = slot_width * neighbors
    device_count = lax.axis_size(AXES)
    capacity = max(2, 2 * row_count // device_count)
    width = design_rows
    waves = [size for size in (capacity // 2, capacity // 4, capacity - capacity // 2 - capacity // 4) if size]

    owners = row_owner[:, 0]
    same_owner = owners[:, None] == owners[None, :]
    row_at = lax.broadcasted_iota(jnp.int32, (row_count, row_count), 0)
    other_at = lax.broadcasted_iota(jnp.int32, (row_count, row_count), 1)
    reaches = row_offset == BLK_DEV - 1
    ahead = jnp.where(reaches[:, None] == reaches[None, :], other_at < row_at, reaches[None, :])
    position = jnp.sum((same_owner & ahead).astype(jnp.int32), axis=1)
    tag = jnp.broadcast_to((row_offset + 1).astype(jnp.bfloat16)[:, None], (row_count, 128))
    payload = jnp.concatenate(
        [
            spline_index.astype(jnp.bfloat16).reshape(row_count, terms * width),
            spline_frac.reshape(row_count, terms * width),
            projection.reshape(row_count, terms * width),
            forces,
            tag,
        ],
        axis=1,
    )

    outgoing = []
    first = 0
    for size in waves:
        slot_at = lax.broadcasted_iota(jnp.int32, (device_count * size, row_count), 0)
        chosen = (slot_at // size == owners[None, :]) & (slot_at % size + first == position[None, :])
        outgoing.append(jnp.dot(chosen.astype(jnp.bfloat16), payload, preferred_element_type=jnp.bfloat16))
        first += size

    def exchange(block):
        return lax.all_to_all(block, AXES, split_axis=0, concat_axis=0, tiled=True)

    def sums(rows, totals, pick):
        where = rows[:, 3 * terms * width + width].astype(jnp.int32)
        return normal_sums(where, rows, terms, width, totals, pick)

    totals = None
    rows = exchange(outgoing[0])
    for block in outgoing[1:]:
        rows, block = lax.optimization_barrier((rows, block))
        coming = exchange(block)
        totals = sums(rows, totals, "all")
        rows = coming
    totals = sums(rows, totals, "last")
    band, rhs = totals
    spill = jnp.concatenate([band[BLK_DEV, 0], rhs[BLK_DEV, 0:1]], axis=0)
    route = [(i, (i + 1) % device_count) for i in range(device_count)]
    spill = lax.ppermute(spill, AXES, route)
    band, rhs = sums(rows, totals, "others")
    normal_band = band[:BLK_DEV].at[0, 0].add(spill[:CO])
    normal_rhs = rhs[:BLK_DEV, 0].at[0].add(spill[CO])
    return (normal_band, normal_rhs)


def solution(mesh):
    split = P(AXES)
    return jax.shard_map(
        on_device, mesh=mesh, in_specs=(split,) * 6, out_specs=(split, split), check_vma=False
    )
```

```python
import functools

import jax
import jax.numpy as jnp
from jax import lax
from jax.experimental import pallas as pl
from jax.experimental.pallas import tpu as pltpu
from jax.sharding import PartitionSpec as P

CO = 128
BLK_DEV = 22
GROUP = 16
ACC_ROWS = BLK_DEV + 3
TRASH = BLK_DEV + 1
HEAD = 16
AXES = ("frame", "panel")


def normal_kernel(neighbors, width, pick, where_ref, rows_ref, *refs):
    if len(refs) == 11:
        band_in, rhs_in = refs[:2]
        refs = refs[2:]
    else:
        band_in = rhs_in = None
    band_ref, rhs_ref, index_ref, weight_ref, force_ref, even_ref, odd_ref, list_ref, block_ref = refs
    slots = where_ref.shape[0]
    lanes = width // 128
    pieces = rows_ref.shape[0] // slots
    span = neighbors * 128

    if band_in is None:
        band_ref[...] = jnp.zeros_like(band_ref)
        rhs_ref[...] = jnp.zeros_like(rhs_ref)
    else:
        band_ref[...] = band_in[...]
        rhs_ref[...] = rhs_in[...]

    def gather_list(slot, count):
        filled = where_ref[slot]
        list_ref[count] = slot
        block_ref[count] = filled - 1
        wanted = filled > 0
        if pick == "last":
            wanted = filled == BLK_DEV
        elif pick == "others":
            wanted = wanted & (filled != BLK_DEV)
        return count + wanted.astype(jnp.int32)

    count = lax.fori_loop(0, slots, gather_list, jnp.int32(0))
    list_ref[count] = 0
    block_ref[count] = TRASH

    @pl.loop(0, jnp.where(count > 0, slots * pieces // GROUP, 0))
    def dense(group):
        at = pl.ds(pl.multiple_of(group * GROUP, GROUP), GROUP)
        for col in range(span // 128):
            index_ref[col, at, :] = rows_ref[at, pl.ds(col * 128, 128)].astype(jnp.float32).astype(jnp.int32)
            t = rows_ref[at, pl.ds(span + col * 128, 128)].astype(jnp.float32)
            p = rows_ref[at, pl.ds(2 * span + col * 128, 128)].astype(jnp.float32) * (1.0 / 6.0)
            one = 1.0 - t
            square = t * t
            cube = square * t
            weight_ref[0, col, at, :] = p * (one * one * one)
            weight_ref[1, col, at, :] = p * (3.0 * cube - 6.0 * square + 4.0)
            weight_ref[2, col, at, :] = p * (3.0 * (square - cube + t) + 1.0)
            weight_ref[3, col, at, :] = p * cube
        force_ref[at, :] = rows_ref[at, pl.ds(3 * span, 128)].astype(jnp.float32)

    sub = lax.broadcasted_iota(jnp.int32, (8, 128), 0)

    def build(slot, design_ref):
        base = slot * pieces
        for lane in range(lanes):
            force = jnp.broadcast_to(force_ref[pl.ds(base + lane, 1), :], (HEAD, 128)).astype(jnp.bfloat16)
            design_ref[0:HEAD, lane * 128 : lane * 128 + 128] = force
        for s in range(2):
            for lane in range(lanes):
                at = pl.ds(base + s * lanes + lane, 1)
                tiles = [None] * (CO // 8)
                for col in range(neighbors):
                    index = jnp.broadcast_to(index_ref[col, at, :], (8, 128))
                    m = (sub - index) & 7
                    value = jnp.where(m == 3, jnp.broadcast_to(weight_ref[3, col, at, :], (8, 128)), 0.0)
                    for k in (2, 1, 0):
                        value = jnp.where(m == k, jnp.broadcast_to(weight_ref[k, col, at, :], (8, 128)), value)
                    target = (index + m) >> 3
                    for a in range(CO // 8):
                        part = jnp.where(target == a, value, 0.0)
                        tiles[a] = part if tiles[a] is None else tiles[a] + part
                for a in range(0, CO // 8, 2):
                    pair = jnp.concatenate([tiles[a], tiles[a + 1]], axis=0).astype(jnp.bfloat16)
                    design_ref[HEAD + s * CO + a * 8 : HEAD + s * CO + a * 8 + 16, lane * 128 : lane * 128 + 128] = pair

    contract = (((1,), (1,)), ((), ()))

    def add(block, design_ref):
        top = lax.dot_general(
            design_ref[0 : HEAD + CO, :], design_ref[HEAD:, :], contract, preferred_element_type=jnp.float32
        )
        low = lax.dot_general(
            design_ref[HEAD + CO :, :], design_ref[HEAD + CO :, :], contract, preferred_element_type=jnp.float32
        )
        band_ref[block, 0] += top[HEAD:, :CO]
        band_ref[block, 1] += top[HEAD:, CO:]
        band_ref[block + 1, 0] += low
        rhs_ref[block] += top[0:8, :CO]
        rhs_ref[block + 1] += top[0:8, CO:]

    odd_ref[...] = jnp.zeros_like(odd_ref)

    def pair(step, before):
        first = 2 * step
        build(list_ref[first], even_ref)
        add(before, odd_ref)
        build(list_ref[first + 1], odd_ref)
        add(block_ref[first], even_ref)
        return block_ref[first + 1]

    last = lax.fori_loop(0, (count + 1) // 2, pair, jnp.int32(TRASH))
    add(last, odd_ref)


def normal_sums(where, rows, neighbors, width, totals, pick):
    slots = where.shape[0]
    held = rows.shape[0]
    vmem = pl.BlockSpec(memory_space=pltpu.VMEM)
    smem = pl.BlockSpec(memory_space=pltpu.SMEM)
    carried = () if totals is None else totals
    return pl.pallas_call(
        functools.partial(normal_kernel, neighbors, width, pick),
        out_shape=(
            jax.ShapeDtypeStruct((ACC_ROWS, 2, CO, CO), jnp.float32),
            jax.ShapeDtypeStruct((ACC_ROWS, 8, CO), jnp.float32),
        ),
        in_specs=[smem, vmem] + [vmem] * len(carried),
        out_specs=(vmem, vmem),
        scratch_shapes=[
            pltpu.VMEM((neighbors, held, 128), jnp.int32),
            pltpu.VMEM((4, neighbors, held, 128), jnp.float32),
            pltpu.VMEM((held, 128), jnp.float32),
            pltpu.VMEM((HEAD + 2 * CO, width), jnp.bfloat16),
            pltpu.VMEM((HEAD + 2 * CO, width), jnp.bfloat16),
            pltpu.SMEM((slots + 8,), jnp.int32),
            pltpu.SMEM((slots + 8,), jnp.int32),
        ],
        compiler_params=pltpu.CompilerParams(vmem_limit_bytes=40 * 1024 * 1024),
        cost_estimate=pl.CostEstimate(
            flops=slots * 20 * 1000 * 1000 * width // 256, bytes_accessed=10 * 1000 * 1000, transcendentals=0
        ),
    )(where, rows, *carried)


def send_kernel(parts, waves, *refs):
    index_ref, frac_ref, proj_ref, force_ref, owner_col, offset_col, owner_row, offset_row = refs[:8]
    out_refs, payload_ref = refs[8:-1], refs[-1]
    slot_width, neighbors, lanes = parts
    pieces = slot_width * lanes
    count = index_ref.shape[0]
    for s in range(slot_width):
        for lane in range(lanes):
            piece = s * lanes + lane
            at = slice(piece * count, (piece + 1) * count)
            for kind, ref in enumerate((index_ref, frac_ref, proj_ref)):
                for n in range(neighbors):
                    source = ((s * neighbors + n) * lanes + lane) * 128
                    column = (kind * neighbors + n) * 128
                    payload_ref[at, column : column + 128] = ref[:, source : source + 128]
            column = 3 * neighbors * 128
            if s == 0:
                payload_ref[at, column : column + 128] = force_ref[:, lane * 128 : lane * 128 + 128]
            else:
                tag = jnp.broadcast_to((offset_col[...] + 1).astype(jnp.float32), (count, 128))
                payload_ref[at, column : column + 128] = tag.astype(jnp.bfloat16)

    shape = (count, count)
    other_at = lax.broadcasted_iota(jnp.int32, shape, 0)
    row_at = lax.broadcasted_iota(jnp.int32, shape, 1)
    other_key = jnp.where(offset_col[...] == BLK_DEV - 1, 0, count) + other_at
    row_key = jnp.where(offset_row[...] == BLK_DEV - 1, 0, count) + row_at
    before = (owner_col[...] == owner_row[...]) & (other_key < row_key)
    position = jnp.sum(jnp.where(before, 1.0, 0.0), axis=0, keepdims=True).astype(jnp.int32)

    first = 0
    for size, out_ref in zip(waves, out_refs):
        inside = (position >= first) & (position < first + size)
        start = owner_row[...] * (size * pieces) + (position - first) * pieces
        target = jnp.concatenate([jnp.where(inside, start + piece, -1) for piece in range(pieces)], axis=1)

        @pl.loop(0, out_ref.shape[0] // 128)
        def place(tile):
            at = pl.multiple_of(tile * 128, 128)
            row_id = lax.broadcasted_iota(jnp.int32, (128, pieces * count), 0) + at
            chosen = jnp.where(row_id == target, 1.0, 0.0).astype(jnp.bfloat16)
            moved = jnp.dot(chosen, payload_ref[...], preferred_element_type=jnp.float32)
            out_ref[pl.ds(at, 128), :] = moved.astype(jnp.bfloat16)

        first += size


def send_blocks(index, frac, proj, forces, owner_col, offset_col, owner_row, offset_row, parts, waves, device_count):
    slot_width, neighbors, lanes = parts
    pieces = slot_width * lanes
    width = (3 * neighbors + 1) * 128
    vmem = pl.BlockSpec(memory_space=pltpu.VMEM)
    return pl.pallas_call(
        functools.partial(send_kernel, parts, waves),
        out_shape=[jax.ShapeDtypeStruct((device_count * size * pieces, width), jnp.bfloat16) for size in waves],
        in_specs=[vmem] * 8,
        out_specs=[vmem] * len(waves),
        scratch_shapes=[pltpu.VMEM((pieces * index.shape[0], width), jnp.bfloat16)],
        compiler_params=pltpu.CompilerParams(vmem_limit_bytes=40 * 1024 * 1024),
    )(index, frac, proj, forces, owner_col, offset_col, owner_row, offset_row)


def on_device(spline_index, spline_frac, projection, forces, row_owner, row_offset):
    row_count, slot_width, neighbors, design_rows = spline_index.shape
    lanes = design_rows // 128
    pieces = slot_width * lanes
    device_count = lax.axis_size(AXES)
    capacity = max(2, 2 * row_count // device_count)
    width = design_rows
    late = max(1, capacity // 4)
    waves = [capacity - late, late]

    flat = (row_count, slot_width * neighbors * design_rows)
    outgoing = send_blocks(
        spline_index.astype(jnp.bfloat16).reshape(flat),
        spline_frac.reshape(flat),
        projection.reshape(flat),
        forces,
        row_owner,
        row_offset[:, None],
        row_owner.reshape(1, row_count),
        row_offset[None, :],
        (slot_width, neighbors, lanes),
        waves,
        device_count,
    )

    def exchange(block):
        return lax.all_to_all(block, AXES, split_axis=0, concat_axis=0, tiled=True)

    def sums(rows, totals, pick):
        where = rows[:, 3 * neighbors * 128].reshape(-1, pieces)[:, pieces - 1].astype(jnp.int32)
        return normal_sums(where, rows, neighbors, width, totals, pick)

    totals = None
    rows = exchange(outgoing[0])
    for block in outgoing[1:]:
        rows, block = lax.optimization_barrier((rows, block))
        coming = exchange(block)
        totals = sums(rows, totals, "all")
        rows = coming
    totals = sums(rows, totals, "last")
    band, rhs = totals
    spill = jnp.concatenate([band[BLK_DEV, 0], rhs[BLK_DEV, 0:1]], axis=0)
    route = [(i, (i + 1) % device_count) for i in range(device_count)]
    spill = lax.ppermute(spill, AXES, route)
    band, rhs = sums(rows, totals, "others")
    normal_band = band[:BLK_DEV].at[0, 0].add(spill[:CO])
    normal_rhs = rhs[:BLK_DEV, 0].at[0].add(spill[CO])
    return (normal_band, normal_rhs)


def solution(mesh):
    split = P(AXES)
    return jax.shard_map(
        on_device, mesh=mesh, in_specs=(split,) * 6, out_specs=(split, split), check_vma=False
    )
```

```python
import functools

import jax
import jax.numpy as jnp
from jax import lax
from jax.experimental import pallas as pl
from jax.experimental.pallas import tpu as pltpu
from jax.sharding import PartitionSpec as P

CO = 128
BLK_DEV = 22
GROUP = 16
ACC_ROWS = BLK_DEV + 3
TRASH = BLK_DEV + 1
HEAD = 16
AXES = ("frame", "panel")


def normal_kernel(neighbors, width, pick, where_ref, rows_ref, *refs):
    if len(refs) == 11:
        band_in, rhs_in = refs[:2]
        refs = refs[2:]
    else:
        band_in = rhs_in = None
    band_ref, rhs_ref, index_ref, weight_ref, force_ref, even_ref, odd_ref, list_ref, block_ref = refs
    slots = where_ref.shape[0]
    lanes = width // 128
    pieces = rows_ref.shape[0] // slots
    span = neighbors * 128

    if band_in is None:
        band_ref[...] = jnp.zeros_like(band_ref)
        rhs_ref[...] = jnp.zeros_like(rhs_ref)
    else:
        band_ref[...] = band_in[...]
        rhs_ref[...] = rhs_in[...]

    def gather_list(slot, count):
        filled = where_ref[slot]
        list_ref[count] = slot
        block_ref[count] = filled - 1
        wanted = filled > 0
        if pick == "last":
            wanted = filled == BLK_DEV
        elif pick == "others":
            wanted = wanted & (filled != BLK_DEV)
        return count + wanted.astype(jnp.int32)

    count = lax.fori_loop(0, slots, gather_list, jnp.int32(0))
    list_ref[count] = 0
    block_ref[count] = TRASH

    @pl.loop(0, jnp.where(count > 0, slots * pieces // GROUP, 0))
    def dense(group):
        at = pl.ds(pl.multiple_of(group * GROUP, GROUP), GROUP)
        for col in range(span // 128):
            index_ref[col, at, :] = rows_ref[at, pl.ds(col * 128, 128)].astype(jnp.float32).astype(jnp.int32)
            t = rows_ref[at, pl.ds(span + col * 128, 128)].astype(jnp.float32)
            p = rows_ref[at, pl.ds(2 * span + col * 128, 128)].astype(jnp.float32) * (1.0 / 6.0)
            one = 1.0 - t
            square = t * t
            cube = square * t
            weight_ref[0, col, at, :] = p * (one * one * one)
            weight_ref[1, col, at, :] = p * (3.0 * cube - 6.0 * square + 4.0)
            weight_ref[2, col, at, :] = p * (3.0 * (square - cube + t) + 1.0)
            weight_ref[3, col, at, :] = p * cube
        force_ref[at, :] = rows_ref[at, pl.ds(3 * span, 128)].astype(jnp.float32)

    sub = lax.broadcasted_iota(jnp.int32, (8, 128), 0)

    def build(slot, design_ref):
        base = slot * pieces
        for lane in range(lanes):
            force = jnp.broadcast_to(force_ref[pl.ds(base + lane, 1), :], (HEAD, 128)).astype(jnp.bfloat16)
            design_ref[0:HEAD, lane * 128 : lane * 128 + 128] = force
        for s in range(2):
            for lane in range(lanes):
                at = pl.ds(base + s * lanes + lane, 1)
                tiles = [None] * (CO // 8)
                for col in range(neighbors):
                    index = jnp.broadcast_to(index_ref[col, at, :], (8, 128))
                    m = (sub - index) & 7
                    value = jnp.where(m == 3, jnp.broadcast_to(weight_ref[3, col, at, :], (8, 128)), 0.0)
                    for k in (2, 1, 0):
                        value = jnp.where(m == k, jnp.broadcast_to(weight_ref[k, col, at, :], (8, 128)), value)
                    target = (index + m) >> 3
                    for a in range(CO // 8):
                        part = jnp.where(target == a, value, 0.0)
                        tiles[a] = part if tiles[a] is None else tiles[a] + part
                for a in range(0, CO // 8, 2):
                    pair = jnp.concatenate([tiles[a], tiles[a + 1]], axis=0).astype(jnp.bfloat16)
                    design_ref[HEAD + s * CO + a * 8 : HEAD + s * CO + a * 8 + 16, lane * 128 : lane * 128 + 128] = pair

    contract = (((1,), (1,)), ((), ()))

    def add(block, design_ref):
        top = lax.dot_general(
            design_ref[0 : HEAD + CO, :], design_ref[HEAD:, :], contract, preferred_element_type=jnp.float32
        )
        low = lax.dot_general(
            design_ref[HEAD + CO :, :], design_ref[HEAD + CO :, :], contract, preferred_element_type=jnp.float32
        )
        band_ref[block, 0] += top[HEAD:, :CO]
        band_ref[block, 1] += top[HEAD:, CO:]
        band_ref[block + 1, 0] += low
        rhs_ref[block] += top[0:8, :CO]
        rhs_ref[block + 1] += top[0:8, CO:]

    odd_ref[...] = jnp.zeros_like(odd_ref)

    def pair(step, before):
        first = 2 * step
        build(list_ref[first], even_ref)
        add(before, odd_ref)
        build(list_ref[first + 1], odd_ref)
        add(block_ref[first], even_ref)
        return block_ref[first + 1]

    last = lax.fori_loop(0, (count + 1) // 2, pair, jnp.int32(TRASH))
    add(last, odd_ref)


def normal_sums(where, rows, neighbors, width, totals, pick):
    slots = where.shape[0]
    held = rows.shape[0]
    vmem = pl.BlockSpec(memory_space=pltpu.VMEM)
    smem = pl.BlockSpec(memory_space=pltpu.SMEM)
    carried = () if totals is None else totals
    return pl.pallas_call(
        functools.partial(normal_kernel, neighbors, width, pick),
        out_shape=(
            jax.ShapeDtypeStruct((ACC_ROWS, 2, CO, CO), jnp.float32),
            jax.ShapeDtypeStruct((ACC_ROWS, 8, CO), jnp.float32),
        ),
        in_specs=[smem, vmem] + [vmem] * len(carried),
        out_specs=(vmem, vmem),
        scratch_shapes=[
            pltpu.VMEM((neighbors, held, 128), jnp.int32),
            pltpu.VMEM((4, neighbors, held, 128), jnp.float32),
            pltpu.VMEM((held, 128), jnp.float32),
            pltpu.VMEM((HEAD + 2 * CO, width), jnp.bfloat16),
            pltpu.VMEM((HEAD + 2 * CO, width), jnp.bfloat16),
            pltpu.SMEM((slots + 8,), jnp.int32),
            pltpu.SMEM((slots + 8,), jnp.int32),
        ],
        compiler_params=pltpu.CompilerParams(vmem_limit_bytes=20 * 1024 * 1024),
        cost_estimate=pl.CostEstimate(
            flops=slots * 20 * 1000 * 1000 * width // 256, bytes_accessed=10 * 1000 * 1000, transcendentals=0
        ),
    )(where, rows, *carried)


def send_kernel(parts, waves, *refs):
    index_ref, frac_ref, proj_ref, force_ref, owner_row, offset_row = refs[:6]
    out_refs, payload_ref = refs[6:-1], refs[-1]
    slot_width, neighbors, lanes = parts
    pieces = slot_width * lanes
    count = index_ref.shape[0]
    shape = (count, count)
    owner_col = jnp.broadcast_to(owner_row[...].astype(jnp.float32), shape).T
    offset_col = jnp.broadcast_to(offset_row[...].astype(jnp.float32), shape).T
    tag = (offset_col[:, :128] + 1.0).astype(jnp.bfloat16)
    for s in range(slot_width):
        for lane in range(lanes):
            piece = s * lanes + lane
            at = slice(piece * count, (piece + 1) * count)
            for kind, ref in enumerate((index_ref, frac_ref, proj_ref)):
                for n in range(neighbors):
                    source = ((s * neighbors + n) * lanes + lane) * 128
                    column = (kind * neighbors + n) * 128
                    payload_ref[at, column : column + 128] = ref[:, source : source + 128]
            column = 3 * neighbors * 128
            if s == 0:
                payload_ref[at, column : column + 128] = force_ref[:, lane * 128 : lane * 128 + 128]
            else:
                payload_ref[at, column : column + 128] = tag

    other_at = lax.broadcasted_iota(jnp.int32, shape, 0)
    row_at = lax.broadcasted_iota(jnp.int32, shape, 1)
    other_key = jnp.where(offset_col == BLK_DEV - 1, 0, count) + other_at
    row_key = jnp.where(offset_row[...] == BLK_DEV - 1, 0, count) + row_at
    before = (owner_col == owner_row[...].astype(jnp.float32)) & (other_key < row_key)
    position = jnp.sum(jnp.where(before, 1.0, 0.0), axis=0, keepdims=True).astype(jnp.int32)

    first = 0
    for size, out_ref in zip(waves, out_refs):
        inside = (position >= first) & (position < first + size)
        start = owner_row[...] * (size * pieces) + (position - first) * pieces
        target = jnp.concatenate([jnp.where(inside, start + piece, -1) for piece in range(pieces)], axis=1)

        @pl.loop(0, out_ref.shape[0] // 128)
        def place(tile):
            at = pl.multiple_of(tile * 128, 128)
            row_id = lax.broadcasted_iota(jnp.int32, (128, pieces * count), 0) + at
            chosen = jnp.where(row_id == target, 1.0, 0.0).astype(jnp.bfloat16)
            moved = jnp.dot(chosen, payload_ref[...], preferred_element_type=jnp.float32)
            out_ref[pl.ds(at, 128), :] = moved.astype(jnp.bfloat16)

        first += size


def send_blocks(index, frac, proj, forces, owner_row, offset_row, parts, waves, device_count):
    slot_width, neighbors, lanes = parts
    pieces = slot_width * lanes
    width = (3 * neighbors + 1) * 128
    vmem = pl.BlockSpec(memory_space=pltpu.VMEM)
    return pl.pallas_call(
        functools.partial(send_kernel, parts, waves),
        out_shape=[jax.ShapeDtypeStruct((device_count * size * pieces, width), jnp.bfloat16) for size in waves],
        in_specs=[vmem] * 6,
        out_specs=[vmem] * len(waves),
        scratch_shapes=[pltpu.VMEM((pieces * index.shape[0], width), jnp.bfloat16)],
        compiler_params=pltpu.CompilerParams(vmem_limit_bytes=20 * 1024 * 1024),
    )(index, frac, proj, forces, owner_row, offset_row)


def on_device(spline_index, spline_frac, projection, forces, row_owner, row_offset):
    row_count, slot_width, neighbors, design_rows = spline_index.shape
    lanes = design_rows // 128
    pieces = slot_width * lanes
    device_count = lax.axis_size(AXES)
    capacity = max(2, 2 * row_count // device_count)
    width = design_rows
    late = max(1, capacity // 4)
    waves = [capacity - late, late]

    flat = (row_count, slot_width * neighbors * design_rows)
    outgoing = send_blocks(
        spline_index.astype(jnp.bfloat16).reshape(flat),
        spline_frac.reshape(flat),
        projection.reshape(flat),
        forces,
        row_owner.reshape(1, row_count),
        row_offset[None, :],
        (slot_width, neighbors, lanes),
        waves,
        device_count,
    )

    def exchange(block):
        return lax.all_to_all(block, AXES, split_axis=0, concat_axis=0, tiled=True)

    def sums(rows, totals, pick):
        where = rows[:, 3 * neighbors * 128].reshape(-1, pieces)[:, pieces - 1].astype(jnp.int32)
        return normal_sums(where, rows, neighbors, width, totals, pick)

    totals = None
    rows = exchange(outgoing[0])
    for block in outgoing[1:]:
        rows, block = lax.optimization_barrier((rows, block))
        coming = exchange(block)
        totals = sums(rows, totals, "all")
        rows = coming
    totals = sums(rows, totals, "last")
    band, rhs = totals
    spill = jnp.concatenate([band[BLK_DEV, 0], rhs[BLK_DEV, 0:1]], axis=0)
    route = [(i, (i + 1) % device_count) for i in range(device_count)]
    spill = lax.ppermute(spill, AXES, route)
    band, rhs = sums(rows, totals, "others")
    normal_band = band[:BLK_DEV].at[0, 0].add(spill[:CO])
    normal_rhs = rhs[:BLK_DEV, 0].at[0].add(spill[CO])
    return (normal_band, normal_rhs)


def solution(mesh):
    split = P(AXES)
    return jax.shard_map(
        on_device, mesh=mesh, in_specs=(split,) * 6, out_specs=(split, split), check_vma=False
    )
```
